32 devices in a mesh: fsdp: 8 (over z, y), seq: 4 (over x, core).
Axes of the slice: x: 2, y: 2, z: 4, core: 2. Of those that a mesh axis runs over, the one named last changes fastest.
Arguments:
- draft_tokens: bfloat16 [8192, 2048], P('fsdp'), may hold values from -6 to 6
- draft_gate: bfloat16 [2048, 4096], P('fsdp', 'seq'), may hold values from -0.125 to 0.125
- draft_up: bfloat16 [2048, 4096], P('fsdp', 'seq'), may hold values from -0.125 to 0.125
- draft_head: float32 [4096], P('seq'), may hold values from -0.75 to 0.75
- verifier_rows: bfloat16 [8192, 8192], P(('fsdp', 'seq')), may hold values from -6 to 6
- norm_gain: float32 [8192], replicated, may hold values from 0.5 to 1.5
- key_weight: bfloat16 [8192, 512], P('fsdp'), may hold values from -0.06629126 to 0.06629126
- value_weight: bfloat16 [8192, 512], P('fsdp'), may hold values from -0.0625 to 0.0625
- pool_query: float32 [4, 4, 128], replicated, may hold values from -32 to 32
- flags: int32 [256], P(('fsdp', 'seq')), may hold values from 0 to 1, as said below
- owner: int32 [256], P(('fsdp', 'seq')), may hold values from 0 to 3
Outputs:
- draft_score: float32 [256], P(('fsdp', 'seq'))
- verdict: bfloat16 [256, 512], P(('fsdp', 'seq'))
The draws below stay inside these ranges and needn't reach their ends.
Inputs may be any that keep to these rules, and one draw needn't show every extreme that they name: `flags`: on the 8 segments of one device, at most 4 flagged segments share an owner lane, and on every device exactly 4 flagged segments share one lane.
All inputs are finite; a program needn't handle non-finite values.
Results may differ from the reference program's by a relative error of at most 0.009.
Values may be sent and summed in bfloat16 or wider, within the bound.
A program may use at most 128 MiB of HBM per device.

```python
import math
import jax
import jax.numpy as jnp
from jax import lax

DD = 2048
DFF = 4096
DV = 8192
KVH = 4
HD = 128
CATS = 4
SEGL = 32
SEG_DEV = 8
CAP = 4
REQ_SEGS = 32
SEGS = 256
N_FSDP = 8


def routing_pair(key):
    blocks = SEGS // SEG_DEV
    key_base = jax.random.fold_in(key, 11)
    key_extra = jax.random.fold_in(key, 12)
    key_shift = jax.random.fold_in(key, 13)
    key_first = jax.random.fold_in(key, 14)
    key_want = jax.random.fold_in(key, 15)
    base = jax.random.randint(key_base, (blocks, SEG_DEV), 0, CATS)
    extra = jax.random.randint(key_extra, (blocks, SEG_DEV), 0, CATS)
    shift = jax.random.randint(key_shift, (blocks, 1), 0, CATS)
    lanes = (jnp.minimum(base, extra) + shift) % CATS
    first_lane = jax.random.randint(key_first, (blocks, 1), 0, CATS)
    position = jnp.arange(SEG_DEV, dtype=jnp.int32)
    forced = position[None, :] < CAP
    lanes = jnp.where(forced, first_lane, lanes)
    wanted = (jax.random.randint(key_want, (blocks, SEG_DEV), 0, 4) > 0) | forced
    earlier = (lanes[:, :, None] == lanes[:, None, :]) & wanted[:, None, :] & (position[None, None, :] < position[None, :, None])
    ranking = jnp.sum(earlier.astype(jnp.int32), axis=2)
    chosen = (wanted & (ranking < CAP)).astype(jnp.int32)
    return (chosen.reshape(SEGS), lanes.astype(jnp.int32).reshape(SEGS))


def draw_flags(key, part):
    return routing_pair(key)[0]


def draw_owner(key, part):
    return routing_pair(key)[1]


def draw_verifier_rows(key, part):
    rows_total = SEGS * SEGL
    key_rows = jax.random.fold_in(key, 31)
    rows = jnp.clip(jax.random.normal(key_rows, (rows_total, DV), jnp.float32), -6.0, 6.0)
    return rows.astype(jnp.bfloat16)


def draw_key_weight(key, part):
    key_main = jax.random.fold_in(key, 41)
    bound = 6.0 * DV ** (-0.5)
    weights = jnp.clip(jax.random.normal(key_main, (DV, KVH * HD), jnp.float32) * DV ** (-0.5), -bound, bound)
    return weights.astype(jnp.bfloat16)


def draw_pool_query(key, part):
    key_main = jax.random.fold_in(key, 51)
    query = jnp.clip(jax.random.normal(key_main, (CATS, KVH, HD), jnp.float32), -6.0, 6.0)
    return query


def steps_of(key, dims, pieces, least, top_value):
    def one(dim, blocks):
        draws = jax.random.uniform(jax.random.fold_in(jax.random.fold_in(key, 6), dim), (blocks,), jnp.float32, least / len(pieces), top_value / len(pieces))
        return jnp.repeat(jnp.exp(draws), dims[dim] // blocks).reshape((-1,) + (1,) * (len(dims) - dim - 1))

    factor_of = one(*pieces[0])
    for cut in pieces[1:]:
        factor_of = factor_of * one(*cut)
    return factor_of


def centred(stream_key, shape, spread, most, cuts=(), held_as=jnp.bfloat16):
    gain = steps_of(stream_key, shape, cuts, -0.22, 0.18) if cuts else 1.0
    array = jax.random.normal(stream_key, shape, jnp.float32) * spread * gain
    return jnp.minimum(jnp.maximum(array, -most), most).astype(held_as)


def setup_inputs(seed: int = 0) -> dict:
    seeds = jax.random.split(jax.random.key(seed), 12)
    draft_tokens = centred(seeds[0], (SEGS * SEGL, DD), 1.0, 6.0, ((0, 8),))
    draft_gate = centred(seeds[1], (DD, DFF), DD ** -0.5, 0.125, ((0, 8), (1, 4)))
    draft_up = centred(seeds[2], (DD, DFF), DD ** -0.5, 0.125, ((0, 8), (1, 4)))
    draft_head = centred(seeds[3], (DFF,), (DFF // 64) ** -0.5, 0.75, ((0, 4),), jnp.float32)
    verifier_rows = draw_verifier_rows(jax.random.fold_in(seeds[11], 71), 0)
    norm_gain = jnp.clip(1.0 + 0.1 * jax.random.normal(seeds[5], (DV,), jnp.float32), 0.5, 1.5)
    key_weight = draw_key_weight(jax.random.fold_in(seeds[11], 71), 0)
    value_weight = centred(seeds[7], (DV, KVH * HD), DV ** -0.5, 0.0625, ((0, 8),))
    pool_query = draw_pool_query(jax.random.fold_in(seeds[11], 71), 0)
    flags = draw_flags(jax.random.fold_in(seeds[11], 71), 0)
    owner = draw_owner(jax.random.fold_in(seeds[11], 71), 0)
    return dict(draft_tokens=draft_tokens, draft_gate=draft_gate, draft_up=draft_up, draft_head=draft_head, verifier_rows=verifier_rows, norm_gain=norm_gain, key_weight=key_weight, value_weight=value_weight, pool_query=pool_query, flags=flags, owner=owner)


eps = 1e-05

def normalize_rows(rows, norm_gain):
    values = rows.astype(jnp.float32)
    scale = lax.rsqrt(lax.optimization_barrier(jnp.mean(values * values, axis=-1, keepdims=True)) + eps)
    return (values * scale * norm_gain).astype(jnp.bfloat16)

def segment_pool(seg_keys, seg_values, queries, head_size):
    scores = jnp.einsum('sthd,shd->sth', seg_keys, queries, precision=lax.Precision.HIGHEST) / math.sqrt(head_size)
    scores = scores - lax.optimization_barrier(jnp.max(scores, axis=1, keepdims=True))
    weights = jnp.exp(scores)
    weights = weights / lax.optimization_barrier(jnp.sum(weights, axis=1, keepdims=True))
    summary_key = jnp.einsum('sth,sthd->shd', weights, seg_keys, precision=lax.Precision.HIGHEST)
    summary_value = jnp.einsum('sth,sthd->shd', weights, seg_values, precision=lax.Precision.HIGHEST)
    return (summary_key, summary_value)

def cross_pool(query_keys, key_all, value_all, live_all, head_size):
    scores = jnp.einsum('jhd,ihd->jhi', query_keys, key_all, precision=lax.Precision.HIGHEST) / math.sqrt(head_size)
    scores = jnp.where(live_all[None, None, :], scores, -1e+30)
    highest = lax.optimization_barrier(jnp.max(scores, axis=2, keepdims=True))
    weights = jnp.where(live_all[None, None, :], jnp.exp(scores - highest), 0.0)
    total = lax.optimization_barrier(jnp.sum(weights, axis=2, keepdims=True))
    return jnp.einsum('jhi,ihd->jhd', weights, value_all, precision=lax.Precision.HIGHEST) / total

def reference(draft_tokens, draft_gate, draft_up, draft_head, verifier_rows, norm_gain, key_weight, value_weight, pool_query, flags, owner):
    blocks = draft_tokens.reshape(N_FSDP, REQ_SEGS * SEGL, DD)

    def draft_block(rows):
        gate = jnp.dot(rows, draft_gate, preferred_element_type=jnp.float32)
        upward = jnp.dot(rows, draft_up, preferred_element_type=jnp.float32)
        return lax.optimization_barrier(jnp.sum(jax.nn.silu(gate) * upward * draft_head, axis=1))
    token_score = lax.map(draft_block, blocks).reshape(SEGS, SEGL)
    draft_score = lax.optimization_barrier(jnp.mean(token_score, axis=1))

    def verify_request(item):
        rows, live_flags, lanes = item
        normed = normalize_rows(rows, norm_gain)
        seg_keys = jnp.dot(normed, key_weight, preferred_element_type=jnp.float32).reshape(REQ_SEGS, SEGL, KVH, HD)
        seg_values = jnp.dot(normed, value_weight, preferred_element_type=jnp.float32).reshape(REQ_SEGS, SEGL, KVH, HD)
        queries = pool_query[lanes]
        summary_key, summary_value = segment_pool(seg_keys, seg_values, queries, HD)
        pooled = cross_pool(summary_key, summary_key, summary_value, live_flags == 1, HD)
        return pooled.reshape(REQ_SEGS, KVH * HD)
    pooled = lax.map(verify_request, (verifier_rows.reshape(N_FSDP, REQ_SEGS * SEGL, DV), flags.reshape(N_FSDP, REQ_SEGS), owner.reshape(N_FSDP, REQ_SEGS)))
    pooled = pooled.reshape(SEGS, KVH * HD)
    verdict = jnp.where(flags[:, None] == 1, jax.nn.sigmoid(draft_score)[:, None] * pooled, 0.0).astype(jnp.bfloat16)
    return (draft_score, verdict)
```

```python
import functools
import math

import jax
import jax.numpy as jnp
from jax import lax
from jax.experimental import pallas as pl
from jax.experimental.pallas import tpu as pltpu
from jax.sharding import PartitionSpec as P

KVH = 4
HD = 128
SEGL = 32


eps = 1e-05


def normalize_rows(rows, norm_gain):
    values = rows.astype(jnp.float32)
    scale = lax.rsqrt(jnp.mean(values * values, axis=-1, keepdims=True) + eps)
    return (values * scale * norm_gain).astype(jnp.bfloat16)


def split_pair(values):
    high = lax.reduce_precision(values, 8, 7)
    return high.astype(jnp.bfloat16), (values - high).astype(jnp.bfloat16)


def pooled_summaries(normed, key_weight, value_weight, pool_query, owner):
    lanes = pool_query.shape[0]
    segs = owner.shape[0]
    groups = lax.axis_size("fsdp")
    depth = key_weight.shape[0]
    key_heads = key_weight.reshape(depth, KVH, HD)
    value_heads = value_weight.reshape(depth, KVH, HD)
    turned = jnp.einsum(
        "chk,dhk->chd",
        pool_query,
        key_heads.astype(jnp.float32),
        precision=lax.Precision.HIGHEST,
    ).reshape(lanes * KVH, depth) / math.sqrt(HD)
    turned = lax.all_gather(turned, "fsdp", axis=0)
    turned = turned.transpose(1, 0, 2).reshape(lanes * KVH, groups * depth)
    both = lax.dot_general(
        normed,
        jnp.concatenate(split_pair(turned), axis=0),
        (((1,), (1,)), ((), ())),
        preferred_element_type=jnp.float32,
    )
    scores = (both[:, : lanes * KVH] + both[:, lanes * KVH :]).reshape(segs, SEGL, lanes, KVH)
    pick = owner[:, None] == jnp.arange(lanes, dtype=jnp.int32)[None, :]
    scores = jnp.sum(jnp.where(pick[:, None, :, None], scores, 0.0), axis=2)
    scores = scores - jnp.max(scores, axis=1, keepdims=True)
    weights = jnp.exp(scores)
    weights = weights / jnp.sum(weights, axis=1, keepdims=True)
    spread = jnp.eye(segs, dtype=jnp.float32)[:, None, :, None] * jnp.transpose(
        weights, (2, 0, 1)
    ).transpose(1, 0, 2)[:, :, None, :]
    spread = spread.reshape(segs * KVH, segs * SEGL)
    high, low = split_pair(spread)
    pools = jnp.dot(jnp.concatenate([high, low], axis=0), normed, preferred_element_type=jnp.float32)
    pools = (pools[: segs * KVH] + pools[segs * KVH :]).astype(jnp.bfloat16)
    pools = pools.reshape(segs * KVH, groups, depth).transpose(1, 0, 2)
    pools = lax.all_to_all(pools, "fsdp", 0, 0).reshape(groups * segs, KVH, depth)
    partial = jnp.stack(
        [
            jnp.einsum("ghd,dhk->ghk", pools, heads, preferred_element_type=jnp.float32)
            for heads in (key_heads, value_heads)
        ]
    ).reshape(2, groups, segs, KVH * HD)
    partial = lax.all_to_all(partial.transpose(1, 0, 2, 3), "fsdp", 0, 0)
    summaries = jnp.sum(partial, axis=0).reshape(2, segs, KVH, HD)
    return summaries[0], summaries[1]


def cross_pool(query_keys, key_all, value_all, live_all, head_size):
    scores = jnp.einsum(
        "jhd,ihd->jhi", query_keys, key_all, precision=lax.Precision.HIGHEST
    ) / math.sqrt(head_size)
    scores = jnp.where(live_all[None, None, :], scores, -1e30)
    highest = jnp.max(scores, axis=2, keepdims=True)
    weights = jnp.where(live_all[None, None, :], jnp.exp(scores - highest), 0.0)
    total = jnp.sum(weights, axis=2, keepdims=True)
    return jnp.einsum("jhi,ihd->jhd", weights, value_all, precision=lax.Precision.HIGHEST) / total


def project_pair(row_block, pieces):
    return (
        jnp.dot(row_block, pieces[0], preferred_element_type=jnp.float32),
        jnp.dot(row_block, pieces[1], preferred_element_type=jnp.float32),
    )


def draft_gathered(draft_tokens, draft_gate, draft_up, draft_head, seg_count):
    gate, upward = project_pair(
        draft_tokens,
        (
            lax.all_gather(draft_gate, "fsdp", axis=0, tiled=True),
            lax.all_gather(draft_up, "fsdp", axis=0, tiled=True),
        ),
    )
    partial_scores = jnp.sum(jax.nn.silu(gate) * upward * draft_head[None, :], axis=1)
    own_scores = lax.psum_scatter(partial_scores, "seq", scatter_dimension=0, tiled=True)
    return jnp.mean(own_scores.reshape(seg_count, SEGL), axis=1)


DEPTHS = 4
WIDE = 512


def plane_kernel_body(
    tok_hbm, gate_hbm, up_hbm, head_ref, out_ref,
    tok, wg, wu, sums, gathered,
    tok_sem, first_send, near_send, far_send, arrive,
    tok_send, tok_arrive, sum_send, sum_arrive,
):
    f = lax.axis_index("fsdp")
    s = lax.axis_index("seq")
    z, y = f // 2, f % 2
    x, c = s // 2, s % 2
    weights = (wg, wu)
    rows = tok_hbm.shape[0]
    depth = gate_hbm.shape[0]
    mesh_id = pl.DeviceIdType.MESH

    barrier = pltpu.get_barrier_semaphore()
    peers = []
    for dy in range(2):
        for ds in range(4):
            if dy or ds:
                peers.append((dy, ds, 2 * z + lax.rem(y + dy, 2), lax.rem(s + ds, 4)))
    for _, _, pf, ps in peers:
        pl.semaphore_signal(barrier, inc=1, device_id=(pf, ps), device_id_type=mesh_id)

    @pl.when(z > 0)
    def _():
        pl.semaphore_signal(barrier, inc=1, device_id=(f - 2, s), device_id_type=mesh_id)

    @pl.when(z < DEPTHS - 1)
    def _():
        pl.semaphore_signal(barrier, inc=1, device_id=(f + 2, s), device_id_type=mesh_id)

    @pl.when(jnp.logical_or(z == 0, z == DEPTHS - 1))
    def _():
        pl.semaphore_wait(barrier, 8)

    @pl.when(jnp.logical_and(z > 0, z < DEPTHS - 1))
    def _():
        pl.semaphore_wait(barrier, 9)

    def slot(ref, index):
        return ref.at[pl.ds(pl.multiple_of(index * depth, depth), depth), :]

    def first(half, part):
        source = (gate_hbm, up_hbm)[part].at[:, half * WIDE : (half + 1) * WIDE]
        return pltpu.make_async_remote_copy(
            src_ref=source,
            dst_ref=slot(weights[part], f),
            send_sem=first_send.at[half, part],
            recv_sem=arrive.at[f, part],
            device_id=(2 * z + c, 2 * x + half),
            device_id_type=mesh_id,
        )

    def kept(half, part):
        source = (gate_hbm, up_hbm)[part].at[:, half * WIDE : (half + 1) * WIDE]
        return pltpu.make_async_copy(source, slot(weights[part], f), arrive.at[f, part])

    def is_self(half):
        return jnp.logical_and(c == y, c == half)

    for half in range(2):
        @pl.when(jnp.logical_not(is_self(half)))
        def _():
            for part in range(2):
                first(half, part).start()

        @pl.when(is_self(half))
        def _():
            for part in range(2):
                kept(half, part).start()

    other_f = 2 * z + 1 - y
    chunks = 4
    size = rows // 2 // chunks

    def chunk_rows(core, chunk):
        return pl.multiple_of(core * (rows // 2) + chunk * size, size)

    def tok_across(chunk):
        start = chunk_rows(c, chunk)
        return pltpu.make_async_remote_copy(
            src_ref=tok_hbm.at[pl.ds(start, size), :],
            dst_ref=tok.at[pl.ds(rows + start, size), :],
            send_sem=tok_send.at[0, chunk],
            recv_sem=tok_arrive.at[0, chunk],
            device_id=(other_f, s),
            device_id_type=mesh_id,
        )

    def tok_over(chunk):
        start = rows + chunk_rows(c, chunk)
        return pltpu.make_async_remote_copy(
            src_ref=tok.at[pl.ds(start, size), :],
            dst_ref=tok.at[pl.ds(start, size), :],
            send_sem=tok_send.at[1, chunk],
            recv_sem=tok_arrive.at[1, chunk],
            device_id=(f, 2 * x + 1 - c),
            device_id_type=mesh_id,
        )

    for chunk in range(chunks):
        tok_across(chunk).start()
    own_tokens = pltpu.make_async_copy(tok_hbm, tok.at[pl.ds(0, rows), :], tok_sem)
    own_tokens.start()

    def forward(index, part, step):
        sems = near_send if step < 0 else far_send
        return pltpu.make_async_remote_copy(
            src_ref=slot(weights[part], index),
            dst_ref=slot(weights[part], index),
            send_sem=sems.at[index, part],
            recv_sem=arrive.at[index, part],
            device_id=(f + 2 * step, s),
            device_id_type=mesh_id,
        )

    def arrived(index):
        for part in range(2):
            forward(index, part, 1).wait_recv()

    def both(index, step, wait):
        for part in range(2):
            if wait:
                forward(index, part, step).wait_send()
            else:
                forward(index, part, step).start()

    def turn(distance, flip, wait):
        side = y if flip == 0 else 1 - y
        if distance == 0:
            index = f if flip == 0 else other_f
            if not wait:
                arrived(index)

            @pl.when(z < DEPTHS - 1)
            def _():
                both(index, 1, wait)

            @pl.when(z > 0)
            def _():
                both(index, -1, wait)

            return

        @pl.when(z >= distance)
        def _():
            index = 2 * (z - distance) + side
            if not wait:
                arrived(index)

            @pl.when(z < DEPTHS - 1)
            def _():
                both(index, 1, wait)

        @pl.when(z + distance < DEPTHS)
        def _():
            index = 2 * (z + distance) + side
            if not wait:
                arrived(index)

            @pl.when(z > 0)
            def _():
                both(index, -1, wait)

    order = ((0, 0), (1, 0), (0, 1), (2, 0), (1, 1), (3, 0), (2, 1), (3, 1))
    passed = 0
    for number, (distance, flip) in enumerate(order):
        turn(distance, flip, False)
        if number >= 2 and passed < chunks:
            tok_across(passed).wait_recv()
            tok_over(passed).start()
            passed += 1
    for chunk in range(chunks):
        tok_over(chunk).wait_recv()
    own_tokens.wait()

    tile = 512
    per = rows // 4
    head = head_ref[...]

    @pl.loop(0, 2 * rows // tile)
    def _(step):
        block = tok[pl.ds(pl.multiple_of(step * tile, tile), tile), :]
        gate = jnp.dot(block, wg[...], preferred_element_type=jnp.float32)
        upward = jnp.dot(block, wu[...], preferred_element_type=jnp.float32)
        product = gate / (1.0 + jnp.exp(-gate)) * upward * head
        by_seg = jnp.sum(product.reshape(tile // SEGL, SEGL, WIDE), axis=1)
        lanes = by_seg[:, 0:128]
        for lane in range(1, WIDE // 128):
            lanes = lanes + by_seg[:, lane * 128 : (lane + 1) * 128]
        for piece in range(tile // per):
            sums[(tile // per) * step + piece] = lanes[piece * 8 : (piece + 1) * 8, :]

    def sum_copy(number, dy, pf, ps):
        return pltpu.make_async_remote_copy(
            src_ref=sums.at[4 * dy + ps],
            dst_ref=gathered.at[number],
            send_sem=sum_send.at[number],
            recv_sem=sum_arrive.at[number],
            device_id=(pf, ps),
            device_id_type=mesh_id,
        )

    for number, (dy, ds, pf, ps) in enumerate(peers):
        sum_copy(number, dy, pf, ps).start()
    total = sums[s]
    for number, (dy, ds, pf, ps) in enumerate(peers):
        sum_copy(number, dy, pf, ps).wait_recv()
        total = total + gathered[number]
    out_ref[...] = total

    for half in range(2):
        @pl.when(jnp.logical_not(is_self(half)))
        def _():
            for part in range(2):
                first(half, part).wait_send()
    for chunk in range(chunks):
        tok_across(chunk).wait_send()
        tok_over(chunk).wait_send()
    for distance, flip in order:
        turn(distance, flip, True)
    for number, (dy, ds, pf, ps) in enumerate(peers):
        sum_copy(number, dy, pf, ps).wait_send()


def draft_plane(draft_tokens, draft_gate, draft_up, draft_head):
    rows, width = draft_tokens.shape
    y = lax.axis_index("fsdp") % 2
    x, c = lax.axis_index("seq") // 2, lax.axis_index("seq") % 2
    every = lax.all_gather(draft_head, "seq", axis=0, tiled=True)
    head = lax.dynamic_slice(every, ((2 * x + y) * 2 * WIDE + c * WIDE,), (WIDE,))
    sems = pltpu.SemaphoreType.DMA
    tiles = pl.pallas_call(
        plane_kernel_body,
        out_shape=jax.ShapeDtypeStruct((8, 128), jnp.float32),
        in_specs=[pl.BlockSpec(memory_space=pl.ANY)] * 3
        + [pl.BlockSpec(memory_space=pltpu.VMEM)],
        out_specs=pl.BlockSpec(memory_space=pltpu.VMEM),
        scratch_shapes=[
            pltpu.VMEM((2 * rows, width), jnp.bfloat16),
            pltpu.VMEM((width, WIDE), jnp.bfloat16),
            pltpu.VMEM((width, WIDE), jnp.bfloat16),
            pltpu.VMEM((8, 8, 128), jnp.float32),
            pltpu.VMEM((7, 8, 128), jnp.float32),
            sems,
            sems((2, 2)),
            sems((8, 2)),
            sems((8, 2)),
            sems((8, 2)),
            sems((2, 4)),
            sems((2, 4)),
            sems((7,)),
            sems((7,)),
        ],
        compiler_params=pltpu.CompilerParams(
            collective_id=0, has_side_effects=True, vmem_limit_bytes=40 * 1024 * 1024
        ),
        cost_estimate=pl.CostEstimate(
            flops=4 * 2 * rows * width * WIDE,
            bytes_accessed=24 * 1024 * 1024,
            transcendentals=2 * rows * WIDE,
        ),
    )(draft_tokens, draft_gate, draft_up, head[None, :])
    return jnp.sum(tiles, axis=1) / SEGL


def local(
    plane_kernel,
    draft_tokens,
    draft_gate,
    draft_up,
    draft_head,
    verifier_rows,
    norm_gain,
    key_weight,
    value_weight,
    pool_query,
    flags,
    owner,
):
    seg_count = flags.shape[0]
    if plane_kernel:
        draft_score = draft_plane(draft_tokens, draft_gate, draft_up, draft_head)
    else:
        draft_score = draft_gathered(draft_tokens, draft_gate, draft_up, draft_head, seg_count)
    normed = normalize_rows(verifier_rows, norm_gain)
    summary_key, summary_value = pooled_summaries(
        normed, key_weight, value_weight, pool_query, owner
    )
    live_own = flags.astype(jnp.float32)
    width = KVH * HD
    packed = jnp.concatenate(
        [
            summary_key.reshape(seg_count, width),
            summary_value.reshape(seg_count, width),
            jnp.broadcast_to(live_own[:, None], (seg_count, 128)),
        ],
        axis=1,
    )
    every = lax.all_gather(packed, "seq", axis=0, tiled=True)
    pooled = cross_pool(
        summary_key,
        every[:, :width].reshape(-1, KVH, HD),
        every[:, width : 2 * width].reshape(-1, KVH, HD),
        every[:, 2 * width] > 0.5,
        HD,
    )
    own_pooled = pooled.reshape(seg_count, KVH * HD)
    verdict = jnp.where(
        flags[:, None] == 1, jax.nn.sigmoid(draft_score)[:, None] * own_pooled, 0.0
    ).astype(jnp.bfloat16)
    return (draft_score, verdict)


def solution(mesh):
    plane_kernel = dict(mesh.shape) == {"fsdp": 2 * DEPTHS, "seq": 4}
    return jax.shard_map(
        functools.partial(local, plane_kernel),
        mesh=mesh,
        in_specs=(
            P("fsdp", None),
            P("fsdp", "seq"),
            P("fsdp", "seq"),
            P("seq"),
            P(("fsdp", "seq"), None),
            P(),
            P("fsdp", None),
            P("fsdp", None),
            P(),
            P(("fsdp", "seq")),
            P(("fsdp", "seq")),
        ),
        out_specs=(P(("fsdp", "seq")), P(("fsdp", "seq"), None)),
        check_vma=False,
    )
```

```python
import functools
import math

import jax
import jax.numpy as jnp
from jax import lax
from jax.experimental import pallas as pl
from jax.experimental.pallas import tpu as pltpu
from jax.sharding import PartitionSpec as P

KVH = 4
HD = 128
SEGL = 32


eps = 1e-05


def normalize_rows(rows, norm_gain):
    values = rows.astype(jnp.float32)
    scale = lax.rsqrt(jnp.mean(values * values, axis=-1, keepdims=True) + eps)
    return (values * scale * norm_gain).astype(jnp.bfloat16)


def split_pair(values):
    high = lax.reduce_precision(values, 8, 7)
    return high.astype(jnp.bfloat16), (values - high).astype(jnp.bfloat16)


def query_rows(key_weight, pool_query):
    depth = key_weight.shape[0]
    return jnp.einsum(
        "chk,dhk->chd",
        pool_query,
        key_weight.reshape(depth, KVH, HD).astype(jnp.float32),
        precision=lax.Precision.HIGHEST,
    ).reshape(pool_query.shape[0] * KVH, depth) / math.sqrt(HD)


def pooled_summaries(normed, key_weight, value_weight, pool_query, owner):
    lanes = pool_query.shape[0]
    segs = owner.shape[0]
    groups = lax.axis_size("fsdp")
    depth = key_weight.shape[0]
    key_heads = key_weight.reshape(depth, KVH, HD)
    value_heads = value_weight.reshape(depth, KVH, HD)
    turned = query_rows(key_weight, pool_query)
    turned = lax.all_gather(turned, "fsdp", axis=0)
    turned = turned.transpose(1, 0, 2).reshape(lanes * KVH, groups * depth)
    both = lax.dot_general(
        normed,
        jnp.concatenate(split_pair(turned), axis=0),
        (((1,), (1,)), ((), ())),
        preferred_element_type=jnp.float32,
    )
    scores = (both[:, : lanes * KVH] + both[:, lanes * KVH :]).reshape(segs, SEGL, lanes, KVH)
    pick = owner[:, None] == jnp.arange(lanes, dtype=jnp.int32)[None, :]
    scores = jnp.sum(jnp.where(pick[:, None, :, None], scores, 0.0), axis=2)
    scores = scores - jnp.max(scores, axis=1, keepdims=True)
    weights = jnp.exp(scores)
    weights = weights / jnp.sum(weights, axis=1, keepdims=True)
    spread = jnp.eye(segs, dtype=jnp.float32)[:, None, :, None] * jnp.transpose(
        weights, (2, 0, 1)
    ).transpose(1, 0, 2)[:, :, None, :]
    spread = spread.reshape(segs * KVH, segs * SEGL)
    high, low = split_pair(spread)
    pools = jnp.dot(jnp.concatenate([high, low], axis=0), normed, preferred_element_type=jnp.float32)
    pools = (pools[: segs * KVH] + pools[segs * KVH :]).astype(jnp.bfloat16)
    pools = pools.reshape(segs * KVH, groups, depth).transpose(1, 0, 2)
    pools = lax.all_to_all(pools, "fsdp", 0, 0).reshape(groups * segs, KVH, depth)
    partial = jnp.stack(
        [
            jnp.einsum("ghd,dhk->ghk", pools, heads, preferred_element_type=jnp.float32)
            for heads in (key_heads, value_heads)
        ]
    ).reshape(2, groups, segs, KVH * HD)
    partial = lax.all_to_all(partial.transpose(1, 0, 2, 3), "fsdp", 0, 0)
    summaries = jnp.sum(partial, axis=0).reshape(2, segs, KVH, HD)
    return summaries[0], summaries[1]


def cross_pool(query_keys, key_all, value_all, live_all, head_size):
    scores = jnp.einsum(
        "jhd,ihd->jhi", query_keys, key_all, precision=lax.Precision.HIGHEST
    ) / math.sqrt(head_size)
    scores = jnp.where(live_all[None, None, :], scores, -1e30)
    highest = jnp.max(scores, axis=2, keepdims=True)
    weights = jnp.where(live_all[None, None, :], jnp.exp(scores - highest), 0.0)
    total = jnp.sum(weights, axis=2, keepdims=True)
    return jnp.einsum("jhi,ihd->jhd", weights, value_all, precision=lax.Precision.HIGHEST) / total


def project_pair(row_block, pieces):
    return (
        jnp.dot(row_block, pieces[0], preferred_element_type=jnp.float32),
        jnp.dot(row_block, pieces[1], preferred_element_type=jnp.float32),
    )


def draft_gathered(draft_tokens, draft_gate, draft_up, draft_head, seg_count):
    gate, upward = project_pair(
        draft_tokens,
        (
            lax.all_gather(draft_gate, "fsdp", axis=0, tiled=True),
            lax.all_gather(draft_up, "fsdp", axis=0, tiled=True),
        ),
    )
    partial_scores = jnp.sum(jax.nn.silu(gate) * upward * draft_head[None, :], axis=1)
    own_scores = lax.psum_scatter(partial_scores, "seq", scatter_dimension=0, tiled=True)
    return jnp.mean(own_scores.reshape(seg_count, SEGL), axis=1)


DEPTHS = 4
WIDE = 512


def plane_kernel_body(
    tok_hbm, gate_hbm, up_hbm, head_in, normed, turned, pick, live, kw, vw,
    out_ref, every_ref,
    tok, wg, wu, sums, gathered, head_ref, every_turned, out_pools, pools, parts, back, every,
    tok_sem, first_send, near_send, far_send, arrive,
    tok_send, tok_arrive, sum_send, sum_arrive,
    head_send, head_arrive, col_send, col_arrive, seq_send, seq_arrive,
):
    f = lax.axis_index("fsdp")
    s = lax.axis_index("seq")
    z, y = f // 2, f % 2
    x, c = s // 2, s % 2
    weights = (wg, wu)
    rows = tok_hbm.shape[0]
    depth = gate_hbm.shape[0]
    mesh_id = pl.DeviceIdType.MESH

    barrier = pltpu.get_barrier_semaphore()
    peers = []
    for dy in range(2):
        for ds in range(4):
            if dy or ds:
                peers.append((dy, ds, 2 * z + lax.rem(y + dy, 2), lax.rem(s + ds, 4)))
    columns = [lax.rem(f + d, 8) for d in range(1, 8)]
    for _, _, pf, ps in peers:
        pl.semaphore_signal(barrier, inc=1, device_id=(pf, ps), device_id_type=mesh_id)
    for cf in columns:
        @pl.when(cf // 2 != z)
        def _():
            pl.semaphore_signal(barrier, inc=1, device_id=(cf, s), device_id_type=mesh_id)

    pl.semaphore_wait(barrier, 13)

    def column_copy(kind, number, source, target):
        return pltpu.make_async_remote_copy(
            src_ref=source,
            dst_ref=target,
            send_sem=col_send.at[kind, number],
            recv_sem=col_arrive.at[kind, number],
            device_id=(columns[number], s),
            device_id_type=mesh_id,
        )

    def turned_copy(number):
        return column_copy(0, number, turned, every_turned.at[f])

    def pools_copy(number):
        return column_copy(1, number, out_pools.at[number], pools.at[f])

    def parts_copy(number):
        return column_copy(2, number, parts.at[columns[number]], back.at[f])

    def seq_copy(number):
        return pltpu.make_async_remote_copy(
            src_ref=every.at[s],
            dst_ref=every.at[s],
            send_sem=seq_send.at[number],
            recv_sem=seq_arrive.at[number],
            device_id=(f, lax.rem(s + number + 1, 4)),
            device_id_type=mesh_id,
        )

    def head_copy(half):
        return pltpu.make_async_remote_copy(
            src_ref=head_in.at[:, half * WIDE : (half + 1) * WIDE],
            dst_ref=head_ref,
            send_sem=head_send,
            recv_sem=head_arrive,
            device_id=(f, 2 * x + half),
            device_id_type=mesh_id,
        )

    for half in range(2):
        @pl.when(jnp.logical_and(c == y, c != half))
        def _():
            head_copy(half).start()

        @pl.when(jnp.logical_and(c == y, c == half))
        def _():
            head_ref[...] = head_in[:, half * WIDE : (half + 1) * WIDE]

    for number in range(7):
        turned_copy(number).start()
    every_turned[f] = turned[...]

    segs = 8
    reach = kw.shape[0]
    width = KVH * HD

    def send_pools():
        for number in range(7):
            turned_copy(number).wait_recv()
        both = jnp.zeros((32, segs * SEGL), jnp.float32)
        for j in range(8):
            values = every_turned[j]
            high = values.astype(jnp.bfloat16)
            low = (values - high.astype(jnp.float32)).astype(jnp.bfloat16)
            both = both + lax.dot_general(
                jnp.concatenate([high, low], axis=0),
                normed[:, j * reach : (j + 1) * reach],
                (((1,), (1,)), ((), ())),
                preferred_element_type=jnp.float32,
            )
        scores = (both[:16] + both[16:]) * pick[...]
        scores = jnp.sum(scores.reshape(4, KVH, segs * SEGL), axis=0)
        wide = jnp.concatenate(
            [jnp.broadcast_to(scores[h : h + 1], (segs, segs * SEGL)) for h in range(KVH)],
            axis=0,
        )
        row = lax.broadcasted_iota(jnp.int32, wide.shape, 0) % segs
        inside = lax.broadcasted_iota(jnp.int32, wide.shape, 1) // SEGL == row
        wide = jnp.where(inside, wide, -1e30)
        shares = jnp.where(inside, jnp.exp(wide - jnp.max(wide, axis=1, keepdims=True)), 0.0)
        shares = shares / jnp.sum(shares, axis=1, keepdims=True)
        high = shares.astype(jnp.bfloat16)
        low = (shares - high.astype(jnp.float32)).astype(jnp.bfloat16)
        pair = jnp.concatenate([high, low], axis=0)

        def pool(j):
            block = normed[:, pl.ds(pl.multiple_of(j * reach, reach), reach)]
            result = jnp.dot(pair, block, preferred_element_type=jnp.float32)
            return (result[:32] + result[32:]).astype(jnp.bfloat16)

        for number in range(7):
            out_pools[number] = pool(columns[number])
            pools_copy(number).start()
        pools[f] = pool(f)

    def send_parts():
        for number in range(7):
            pools_copy(number).wait_recv()
        block = pools[...].reshape(8 * 32, reach)
        for which, ref in enumerate((kw, vw)):
            result = jnp.dot(block, ref[...], preferred_element_type=jnp.float32)
            result = result.reshape(8, KVH, segs, width)
            for h in range(KVH):
                start = which * width + h * HD
                parts[:, :, start : start + HD] = result[:, h, :, h * HD : (h + 1) * HD]
        for number in range(7):
            parts_copy(number).start()
        back[f] = parts[f]

    def send_summaries():
        for number in range(7):
            parts_copy(number).wait_recv()
        every[s] = jnp.concatenate([jnp.sum(back[...], axis=0), live[...]], axis=1)
        for number in range(3):
            seq_copy(number).start()

    def slot(ref, index):
        return ref.at[pl.ds(pl.multiple_of(index * depth, depth), depth), :]

    def first(half, part):
        source = (gate_hbm, up_hbm)[part].at[:, half * WIDE : (half + 1) * WIDE]
        return pltpu.make_async_remote_copy(
            src_ref=source,
            dst_ref=slot(weights[part], f),
            send_sem=first_send.at[half, part],
            recv_sem=arrive.at[f, part],
            device_id=(2 * z + c, 2 * x + half),
            device_id_type=mesh_id,
        )

    def kept(half, part):
        source = (gate_hbm, up_hbm)[part].at[:, half * WIDE : (half + 1) * WIDE]
        return pltpu.make_async_copy(source, slot(weights[part], f), arrive.at[f, part])

    def is_self(half):
        return jnp.logical_and(c == y, c == half)

    for half in range(2):
        @pl.when(jnp.logical_not(is_self(half)))
        def _():
            for part in range(2):
                first(half, part).start()

        @pl.when(is_self(half))
        def _():
            for part in range(2):
                kept(half, part).start()

    other_f = 2 * z + 1 - y
    chunks = 4
    size = rows // 2 // chunks

    def chunk_rows(core, chunk):
        return pl.multiple_of(core * (rows // 2) + chunk * size, size)

    def tok_across(chunk):
        start = chunk_rows(c, chunk)
        return pltpu.make_async_remote_copy(
            src_ref=tok_hbm.at[pl.ds(start, size), :],
            dst_ref=tok.at[pl.ds(rows + start, size), :],
            send_sem=tok_send.at[0, chunk],
            recv_sem=tok_arrive.at[0, chunk],
            device_id=(other_f, s),
            device_id_type=mesh_id,
        )

    def tok_over(chunk):
        start = rows + chunk_rows(c, chunk)
        return pltpu.make_async_remote_copy(
            src_ref=tok.at[pl.ds(start, size), :],
            dst_ref=tok.at[pl.ds(start, size), :],
            send_sem=tok_send.at[1, chunk],
            recv_sem=tok_arrive.at[1, chunk],
            device_id=(f, 2 * x + 1 - c),
            device_id_type=mesh_id,
        )

    for chunk in range(chunks):
        tok_across(chunk).start()
    own_tokens = pltpu.make_async_copy(tok_hbm, tok.at[pl.ds(0, rows), :], tok_sem)
    own_tokens.start()

    def forward(index, part, step):
        sems = near_send if step < 0 else far_send
        return pltpu.make_async_remote_copy(
            src_ref=slot(weights[part], index),
            dst_ref=slot(weights[part], index),
            send_sem=sems.at[index, part],
            recv_sem=arrive.at[index, part],
            device_id=(f + 2 * step, s),
            device_id_type=mesh_id,
        )

    def arrived(index):
        for part in range(2):
            forward(index, part, 1).wait_recv()

    def both(index, step, wait):
        for part in range(2):
            if wait:
                forward(index, part, step).wait_send()
            else:
                forward(index, part, step).start()

    def turn(distance, flip, wait):
        side = y if flip == 0 else 1 - y
        if distance == 0:
            index = f if flip == 0 else other_f
            if not wait:
                arrived(index)

            @pl.when(z < DEPTHS - 1)
            def _():
                both(index, 1, wait)

            @pl.when(z > 0)
            def _():
                both(index, -1, wait)

            return

        @pl.when(z >= distance)
        def _():
            index = 2 * (z - distance) + side
            if not wait:
                arrived(index)

            @pl.when(z < DEPTHS - 1)
            def _():
                both(index, 1, wait)

        @pl.when(z + distance < DEPTHS)
        def _():
            index = 2 * (z + distance) + side
            if not wait:
                arrived(index)

            @pl.when(z > 0)
            def _():
                both(index, -1, wait)

    order = ((0, 0), (1, 0), (0, 1), (2, 0), (1, 1), (3, 0), (2, 1), (3, 1))
    passed = 0
    for number, (distance, flip) in enumerate(order):
        turn(distance, flip, False)
        if number == 1:
            send_pools()
        if number == 3:
            send_parts()
        if number == 5:
            send_summaries()
        if number >= 2 and passed < chunks:
            tok_across(passed).wait_recv()
            tok_over(passed).start()
            passed += 1
    for chunk in range(chunks):
        tok_over(chunk).wait_recv()
    own_tokens.wait()

    tile = 512
    per = rows // 4

    @pl.when(c != y)
    def _():
        head_copy(0).wait_recv()

    head = head_ref[0:1, :]

    @pl.loop(0, 2 * rows // tile)
    def _(step):
        block = tok[pl.ds(pl.multiple_of(step * tile, tile), tile), :]
        gate = jnp.dot(block, wg[...], preferred_element_type=jnp.float32)
        upward = jnp.dot(block, wu[...], preferred_element_type=jnp.float32)
        product = gate / (1.0 + jnp.exp(-gate)) * upward * head
        by_seg = jnp.sum(product.reshape(tile // SEGL, SEGL, WIDE), axis=1)
        lanes = by_seg[:, 0:128]
        for lane in range(1, WIDE // 128):
            lanes = lanes + by_seg[:, lane * 128 : (lane + 1) * 128]
        for piece in range(tile // per):
            sums[(tile // per) * step + piece] = lanes[piece * 8 : (piece + 1) * 8, :]

    def sum_copy(number, dy, pf, ps):
        return pltpu.make_async_remote_copy(
            src_ref=sums.at[4 * dy + ps],
            dst_ref=gathered.at[number],
            send_sem=sum_send.at[number],
            recv_sem=sum_arrive.at[number],
            device_id=(pf, ps),
            device_id_type=mesh_id,
        )

    for number, (dy, ds, pf, ps) in enumerate(peers):
        sum_copy(number, dy, pf, ps).start()
    total = sums[s]
    for number, (dy, ds, pf, ps) in enumerate(peers):
        sum_copy(number, dy, pf, ps).wait_recv()
        total = total + gathered[number]
    out_ref[...] = total
    for number in range(3):
        seq_copy(number).wait_recv()
    every_ref[...] = every[...]
    for number in range(7):
        turned_copy(number).wait_send()
        pools_copy(number).wait_send()
        parts_copy(number).wait_send()
    for number in range(3):
        seq_copy(number).wait_send()

    @pl.when(c == y)
    def _():
        head_copy(0).wait_send()

    for half in range(2):
        @pl.when(jnp.logical_not(is_self(half)))
        def _():
            for part in range(2):
                first(half, part).wait_send()
    for chunk in range(chunks):
        tok_across(chunk).wait_send()
        tok_over(chunk).wait_send()
    for distance, flip in order:
        turn(distance, flip, True)
    for number, (dy, ds, pf, ps) in enumerate(peers):
        sum_copy(number, dy, pf, ps).wait_send()


def plane(
    draft_tokens, draft_gate, draft_up, draft_head, normed, key_weight, value_weight,
    pool_query, flags, owner,
):
    rows, width = draft_tokens.shape
    segs = flags.shape[0]
    lanes = pool_query.shape[0]
    depth = key_weight.shape[0]
    turned = query_rows(key_weight, pool_query)
    pick = (jnp.repeat(owner, SEGL)[None, :] == jnp.arange(lanes, dtype=jnp.int32)[:, None])
    pick = jnp.repeat(pick.astype(jnp.float32), KVH, axis=0)
    live = jnp.broadcast_to(flags.astype(jnp.float32)[:, None], (segs, 128))
    head = jnp.broadcast_to(draft_head[None, :], (8, draft_head.shape[0]))
    packed = 2 * KVH * HD + 128
    sems = pltpu.SemaphoreType.DMA
    tiles, every = pl.pallas_call(
        plane_kernel_body,
        out_shape=(
            jax.ShapeDtypeStruct((8, 128), jnp.float32),
            jax.ShapeDtypeStruct((4, segs, packed), jnp.float32),
        ),
        in_specs=[pl.BlockSpec(memory_space=pl.ANY)] * 3
        + [pl.BlockSpec(memory_space=pltpu.VMEM)] * 7,
        out_specs=(pl.BlockSpec(memory_space=pltpu.VMEM),) * 2,
        scratch_shapes=[
            pltpu.VMEM((2 * rows, width), jnp.bfloat16),
            pltpu.VMEM((width, WIDE), jnp.bfloat16),
            pltpu.VMEM((width, WIDE), jnp.bfloat16),
            pltpu.VMEM((8, 8, 128), jnp.float32),
            pltpu.VMEM((7, 8, 128), jnp.float32),
            pltpu.VMEM((8, WIDE), jnp.float32),
            pltpu.VMEM((8, lanes * KVH, depth), jnp.float32),
            pltpu.VMEM((7, KVH * segs, depth), jnp.bfloat16),
            pltpu.VMEM((8, KVH * segs, depth), jnp.bfloat16),
            pltpu.VMEM((8, segs, packed - 128), jnp.float32),
            pltpu.VMEM((8, segs, packed - 128), jnp.float32),
            pltpu.VMEM((4, segs, packed), jnp.float32),
            sems,
            sems((2, 2)),
            sems((8, 2)),
            sems((8, 2)),
            sems((8, 2)),
            sems((2, 4)),
            sems((2, 4)),
            sems((7,)),
            sems((7,)),
            sems,
            sems,
            sems((3, 7)),
            sems((3, 7)),
            sems((3,)),
            sems((3,)),
        ],
        compiler_params=pltpu.CompilerParams(
            collective_id=0, has_side_effects=True, vmem_limit_bytes=48 * 1024 * 1024
        ),
        cost_estimate=pl.CostEstimate(
            flops=4 * 2 * rows * width * WIDE,
            bytes_accessed=24 * 1024 * 1024,
            transcendentals=2 * rows * WIDE,
        ),
    )(
        draft_tokens, draft_gate, draft_up, head, normed, turned, pick, live,
        key_weight, value_weight,
    )
    return jnp.sum(tiles, axis=1) / SEGL, every


def local(
    plane_kernel,
    draft_tokens,
    draft_gate,
    draft_up,
    draft_head,
    verifier_rows,
    norm_gain,
    key_weight,
    value_weight,
    pool_query,
    flags,
    owner,
):
    seg_count = flags.shape[0]
    normed = normalize_rows(verifier_rows, norm_gain)
    width = KVH * HD
    if plane_kernel:
        draft_score, every = plane(
            draft_tokens, draft_gate, draft_up, draft_head, normed, key_weight, value_weight,
            pool_query, flags, owner,
        )
        own = every[lax.axis_index("seq")]
        summary_key = own[:, :width].reshape(seg_count, KVH, HD)
        every = every.reshape(4 * seg_count, 2 * width + 128)
    else:
        draft_score = draft_gathered(draft_tokens, draft_gate, draft_up, draft_head, seg_count)
        summary_key, summary_value = pooled_summaries(
            normed, key_weight, value_weight, pool_query, owner
        )
        packed = jnp.concatenate(
            [
                summary_key.reshape(seg_count, width),
                summary_value.reshape(seg_count, width),
                jnp.broadcast_to(flags.astype(jnp.float32)[:, None], (seg_count, 128)),
            ],
            axis=1,
        )
        every = lax.all_gather(packed, "seq", axis=0, tiled=True)
    pooled = cross_pool(
        summary_key,
        every[:, :width].reshape(-1, KVH, HD),
        every[:, width : 2 * width].reshape(-1, KVH, HD),
        every[:, 2 * width] > 0.5,
        HD,
    )
    own_pooled = pooled.reshape(seg_count, KVH * HD)
    verdict = jnp.where(
        flags[:, None] == 1, jax.nn.sigmoid(draft_score)[:, None] * own_pooled, 0.0
    ).astype(jnp.bfloat16)
    return (draft_score, verdict)


def solution(mesh):
    plane_kernel = dict(mesh.shape) == {"fsdp": 2 * DEPTHS, "seq": 4}
    return jax.shard_map(
        functools.partial(local, plane_kernel),
        mesh=mesh,
        in_specs=(
            P("fsdp", None),
            P("fsdp", "seq"),
            P("fsdp", "seq"),
            P("seq"),
            P(("fsdp", "seq"), None),
            P(),
            P("fsdp", None),
            P("fsdp", None),
            P(),
            P(("fsdp", "seq")),
            P(("fsdp", "seq")),
        ),
        out_specs=(P(("fsdp", "seq")), P(("fsdp", "seq"), None)),
        check_vma=False,
    )
```

```python
import functools
import math

import jax
import jax.numpy as jnp
from jax import lax
from jax.experimental import pallas as pl
from jax.experimental.pallas import tpu as pltpu
from jax.sharding import PartitionSpec as P

KVH = 4
HD = 128
SEGL = 32


eps = 1e-05


def normalize_rows(rows, norm_gain):
    values = rows.astype(jnp.float32)
    scale = lax.rsqrt(jnp.mean(values * values, axis=-1, keepdims=True) + eps)
    return (values * scale * norm_gain).astype(jnp.bfloat16)


def split_pair(values):
    high = lax.reduce_precision(values, 8, 7)
    return high.astype(jnp.bfloat16), (values - high).astype(jnp.bfloat16)


def query_rows(key_weight, pool_query):
    depth = key_weight.shape[0]
    return jnp.einsum(
        "chk,dhk->chd",
        pool_query,
        key_weight.reshape(depth, KVH, HD).astype(jnp.float32),
        precision=lax.Precision.HIGHEST,
    ).reshape(pool_query.shape[0] * KVH, depth) / math.sqrt(HD)


def pooled_summaries(normed, key_weight, value_weight, pool_query, owner):
    lanes = pool_query.shape[0]
    segs = owner.shape[0]
    groups = lax.axis_size("fsdp")
    depth = key_weight.shape[0]
    key_heads = key_weight.reshape(depth, KVH, HD)
    value_heads = value_weight.reshape(depth, KVH, HD)
    turned = query_rows(key_weight, pool_query)
    turned = lax.all_gather(turned, "fsdp", axis=0)
    turned = turned.transpose(1, 0, 2).reshape(lanes * KVH, groups * depth)
    both = lax.dot_general(
        normed,
        jnp.concatenate(split_pair(turned), axis=0),
        (((1,), (1,)), ((), ())),
        preferred_element_type=jnp.float32,
    )
    scores = (both[:, : lanes * KVH] + both[:, lanes * KVH :]).reshape(segs, SEGL, lanes, KVH)
    pick = owner[:, None] == jnp.arange(lanes, dtype=jnp.int32)[None, :]
    scores = jnp.sum(jnp.where(pick[:, None, :, None], scores, 0.0), axis=2)
    scores = scores - jnp.max(scores, axis=1, keepdims=True)
    weights = jnp.exp(scores)
    weights = weights / jnp.sum(weights, axis=1, keepdims=True)
    spread = jnp.eye(segs, dtype=jnp.float32)[:, None, :, None] * jnp.transpose(
        weights, (2, 0, 1)
    ).transpose(1, 0, 2)[:, :, None, :]
    spread = spread.reshape(segs * KVH, segs * SEGL)
    high, low = split_pair(spread)
    pools = jnp.dot(jnp.concatenate([high, low], axis=0), normed, preferred_element_type=jnp.float32)
    pools = (pools[: segs * KVH] + pools[segs * KVH :]).astype(jnp.bfloat16)
    pools = pools.reshape(segs * KVH, groups, depth).transpose(1, 0, 2)
    pools = lax.all_to_all(pools, "fsdp", 0, 0).reshape(groups * segs, KVH, depth)
    partial = jnp.stack(
        [
            jnp.einsum("ghd,dhk->ghk", pools, heads, preferred_element_type=jnp.float32)
            for heads in (key_heads, value_heads)
        ]
    ).reshape(2, groups, segs, KVH * HD)
    partial = lax.all_to_all(partial.transpose(1, 0, 2, 3), "fsdp", 0, 0)
    summaries = jnp.sum(partial, axis=0).reshape(2, segs, KVH, HD)
    return summaries[0], summaries[1]


def cross_pool(query_keys, key_all, value_all, live_all, head_size):
    scores = jnp.einsum(
        "jhd,ihd->jhi", query_keys, key_all, precision=lax.Precision.HIGHEST
    ) / math.sqrt(head_size)
    scores = jnp.where(live_all[None, None, :], scores, -1e30)
    highest = jnp.max(scores, axis=2, keepdims=True)
    weights = jnp.where(live_all[None, None, :], jnp.exp(scores - highest), 0.0)
    total = jnp.sum(weights, axis=2, keepdims=True)
    return jnp.einsum("jhi,ihd->jhd", weights, value_all, precision=lax.Precision.HIGHEST) / total


def project_pair(row_block, pieces):
    return (
        jnp.dot(row_block, pieces[0], preferred_element_type=jnp.float32),
        jnp.dot(row_block, pieces[1], preferred_element_type=jnp.float32),
    )


def draft_gathered(draft_tokens, draft_gate, draft_up, draft_head, seg_count):
    gate, upward = project_pair(
        draft_tokens,
        (
            lax.all_gather(draft_gate, "fsdp", axis=0, tiled=True),
            lax.all_gather(draft_up, "fsdp", axis=0, tiled=True),
        ),
    )
    partial_scores = jnp.sum(jax.nn.silu(gate) * upward * draft_head[None, :], axis=1)
    own_scores = lax.psum_scatter(partial_scores, "seq", scatter_dimension=0, tiled=True)
    return jnp.mean(own_scores.reshape(seg_count, SEGL), axis=1)


DEPTHS = 4
WIDE = 512


def plane_kernel_body(
    tok_hbm, gate_hbm, up_hbm, head_in, normed, turned, pick, live, kw, vw,
    out_ref, every_ref,
    tok, wg, wu, sums, gathered, head_ref, every_turned, out_pools, pools, parts, back, every,
    tok_sem, first_send, near_send, far_send, arrive,
    tok_send, tok_arrive, sum_send, sum_arrive,
    head_send, head_arrive, col_send, col_arrive, seq_send, seq_arrive,
):
    f = lax.axis_index("fsdp")
    s = lax.axis_index("seq")
    z, y = f // 2, f % 2
    x, c = s // 2, s % 2
    weights = (wg, wu)
    rows = tok_hbm.shape[0]
    depth = gate_hbm.shape[0]
    mesh_id = pl.DeviceIdType.MESH

    barrier = pltpu.get_barrier_semaphore()
    peers = []
    for dy in range(2):
        for ds in range(4):
            if dy or ds:
                peers.append((dy, ds, 2 * z + lax.rem(y + dy, 2), lax.rem(s + ds, 4)))
    columns = [lax.rem(f + d, 8) for d in range(1, 8)]
    for _, _, pf, ps in peers:
        pl.semaphore_signal(barrier, inc=1, device_id=(pf, ps), device_id_type=mesh_id)
    for cf in columns:
        @pl.when(cf // 2 != z)
        def _():
            pl.semaphore_signal(barrier, inc=1, device_id=(cf, s), device_id_type=mesh_id)

    pl.semaphore_wait(barrier, 13)

    def column_copy(kind, number, source, target):
        return pltpu.make_async_remote_copy(
            src_ref=source,
            dst_ref=target,
            send_sem=col_send.at[kind, number],
            recv_sem=col_arrive.at[kind, number],
            device_id=(columns[number], s),
            device_id_type=mesh_id,
        )

    def turned_copy(number):
        return column_copy(0, number, turned, every_turned.at[f])

    def pools_copy(number):
        return column_copy(1, number, out_pools.at[number], pools.at[f])

    def parts_copy(number):
        return column_copy(2, number, parts.at[columns[number]], back.at[f])

    def seq_copy(number):
        return pltpu.make_async_remote_copy(
            src_ref=every.at[s],
            dst_ref=every.at[s],
            send_sem=seq_send.at[number],
            recv_sem=seq_arrive.at[number],
            device_id=(f, lax.rem(s + number + 1, 4)),
            device_id_type=mesh_id,
        )

    def head_copy(half):
        return pltpu.make_async_remote_copy(
            src_ref=head_in.at[:, half * WIDE : (half + 1) * WIDE],
            dst_ref=head_ref,
            send_sem=head_send,
            recv_sem=head_arrive,
            device_id=(f, 2 * x + half),
            device_id_type=mesh_id,
        )

    for half in range(2):
        @pl.when(jnp.logical_and(c == y, c != half))
        def _():
            head_copy(half).start()

        @pl.when(jnp.logical_and(c == y, c == half))
        def _():
            head_ref[...] = head_in[:, half * WIDE : (half + 1) * WIDE]

    for number in range(7):
        turned_copy(number).start()
    every_turned[f] = turned[...]

    segs = 8
    reach = kw.shape[0]
    width = KVH * HD

    def send_pools():
        for number in range(7):
            turned_copy(number).wait_recv()
        both = jnp.zeros((32, segs * SEGL), jnp.float32)
        for j in range(8):
            values = every_turned[j]
            high = values.astype(jnp.bfloat16)
            low = (values - high.astype(jnp.float32)).astype(jnp.bfloat16)
            both = both + lax.dot_general(
                jnp.concatenate([high, low], axis=0),
                normed[:, j * reach : (j + 1) * reach],
                (((1,), (1,)), ((), ())),
                preferred_element_type=jnp.float32,
            )
        scores = (both[:16] + both[16:]) * pick[...]
        scores = jnp.sum(scores.reshape(4, KVH, segs * SEGL), axis=0)
        wide = jnp.concatenate(
            [jnp.broadcast_to(scores[h : h + 1], (segs, segs * SEGL)) for h in range(KVH)],
            axis=0,
        )
        row = lax.broadcasted_iota(jnp.int32, wide.shape, 0) % segs
        inside = lax.broadcasted_iota(jnp.int32, wide.shape, 1) // SEGL == row
        wide = jnp.where(inside, wide, -1e30)
        shares = jnp.where(inside, jnp.exp(wide - jnp.max(wide, axis=1, keepdims=True)), 0.0)
        shares = shares / jnp.sum(shares, axis=1, keepdims=True)
        high = shares.astype(jnp.bfloat16)
        low = (shares - high.astype(jnp.float32)).astype(jnp.bfloat16)
        pair = jnp.concatenate([high, low], axis=0)

        def pool(j):
            block = normed[:, pl.ds(pl.multiple_of(j * reach, reach), reach)]
            result = jnp.dot(pair, block, preferred_element_type=jnp.float32)
            return (result[:32] + result[32:]).astype(jnp.bfloat16)

        for number in range(7):
            out_pools[number] = pool(columns[number])
            pools_copy(number).start()
        pools[f] = pool(f)

    def send_parts():
        for number in range(7):
            pools_copy(number).wait_recv()
        block = pools[...].reshape(8 * 32, reach)
        for which, ref in enumerate((kw, vw)):
            result = jnp.dot(block, ref[...], preferred_element_type=jnp.float32)
            result = result.reshape(8, KVH, segs, width)
            for h in range(KVH):
                start = which * width + h * HD
                parts[:, :, start : start + HD] = result[:, h, :, h * HD : (h + 1) * HD]
        for number in range(7):
            parts_copy(number).start()
        back[f] = parts[f]

    def send_summaries():
        for number in range(7):
            parts_copy(number).wait_recv()
        every[s] = jnp.concatenate([jnp.sum(back[...], axis=0), live[...]], axis=1)
        for number in range(3):
            seq_copy(number).start()

    def slot(ref, index):
        return ref.at[pl.ds(pl.multiple_of(index * depth, depth), depth), :]

    def first(half, part):
        source = (gate_hbm, up_hbm)[part].at[:, half * WIDE : (half + 1) * WIDE]
        return pltpu.make_async_remote_copy(
            src_ref=source,
            dst_ref=slot(weights[part], f),
            send_sem=first_send.at[half, part],
            recv_sem=arrive.at[f, part],
            device_id=(2 * z + c, 2 * x + half),
            device_id_type=mesh_id,
        )

    def kept(half, part):
        source = (gate_hbm, up_hbm)[part].at[:, half * WIDE : (half + 1) * WIDE]
        return pltpu.make_async_copy(source, slot(weights[part], f), arrive.at[f, part])

    def is_self(half):
        return jnp.logical_and(c == y, c == half)

    for half in range(2):
        @pl.when(jnp.logical_not(is_self(half)))
        def _():
            for part in range(2):
                first(half, part).start()

        @pl.when(is_self(half))
        def _():
            for part in range(2):
                kept(half, part).start()

    other_f = 2 * z + 1 - y
    chunks = 4
    size = rows // 2 // chunks

    def chunk_rows(core, chunk):
        return pl.multiple_of(core * (rows // 2) + chunk * size, size)

    def tok_across(chunk):
        start = chunk_rows(c, chunk)
        return pltpu.make_async_remote_copy(
            src_ref=tok_hbm.at[pl.ds(start, size), :],
            dst_ref=tok.at[pl.ds(rows + start, size), :],
            send_sem=tok_send.at[0, chunk],
            recv_sem=tok_arrive.at[0, chunk],
            device_id=(other_f, s),
            device_id_type=mesh_id,
        )

    def tok_over(chunk):
        start = rows + chunk_rows(c, chunk)
        return pltpu.make_async_remote_copy(
            src_ref=tok.at[pl.ds(start, size), :],
            dst_ref=tok.at[pl.ds(start, size), :],
            send_sem=tok_send.at[1, chunk],
            recv_sem=tok_arrive.at[1, chunk],
            device_id=(f, 2 * x + 1 - c),
            device_id_type=mesh_id,
        )

    for chunk in range(chunks):
        tok_across(chunk).start()
    own_tokens = pltpu.make_async_copy(tok_hbm, tok.at[pl.ds(0, rows), :], tok_sem)
    own_tokens.start()

    def forward(index, part, step):
        sems = near_send if step < 0 else far_send
        return pltpu.make_async_remote_copy(
            src_ref=slot(weights[part], index),
            dst_ref=slot(weights[part], index),
            send_sem=sems.at[index, part],
            recv_sem=arrive.at[index, part],
            device_id=(f + 2 * step, s),
            device_id_type=mesh_id,
        )

    def arrived(index):
        for part in range(2):
            forward(index, part, 1).wait_recv()

    def both(index, step, wait):
        for part in range(2):
            if wait:
                forward(index, part, step).wait_send()
            else:
                forward(index, part, step).start()

    def turn(distance, flip, wait):
        side = y if flip == 0 else 1 - y
        if distance == 0:
            index = f if flip == 0 else other_f
            if not wait:
                arrived(index)

            @pl.when(z < DEPTHS - 1)
            def _():
                both(index, 1, wait)

            @pl.when(z > 0)
            def _():
                both(index, -1, wait)

            return

        @pl.when(z >= distance)
        def _():
            index = 2 * (z - distance) + side
            if not wait:
                arrived(index)

            @pl.when(z < DEPTHS - 1)
            def _():
                both(index, 1, wait)

        @pl.when(z + distance < DEPTHS)
        def _():
            index = 2 * (z + distance) + side
            if not wait:
                arrived(index)

            @pl.when(z > 0)
            def _():
                both(index, -1, wait)

    order = ((0, 0), (1, 0), (0, 1), (2, 0), (1, 1), (3, 0), (2, 1), (3, 1))
    for number, (distance, flip) in enumerate(order):
        turn(distance, flip, False)
        if number == 1:
            send_pools()
    for chunk in range(chunks):
        tok_across(chunk).wait_recv()
        tok_over(chunk).start()
    send_parts()
    for chunk in range(chunks):
        tok_over(chunk).wait_recv()
    own_tokens.wait()

    tile = 512
    per = rows // 4

    @pl.when(c != y)
    def _():
        head_copy(0).wait_recv()

    head = head_ref[0:1, :]

    @pl.loop(0, 2 * rows // tile)
    def _(step):
        block = tok[pl.ds(pl.multiple_of(step * tile, tile), tile), :]
        gate = jnp.dot(block, wg[...], preferred_element_type=jnp.float32)
        upward = jnp.dot(block, wu[...], preferred_element_type=jnp.float32)
        product = gate / (1.0 + jnp.exp(-gate)) * upward * head
        by_seg = jnp.sum(product.reshape(tile // SEGL, SEGL, WIDE), axis=1)
        lanes = by_seg[:, 0:128]
        for lane in range(1, WIDE // 128):
            lanes = lanes + by_seg[:, lane * 128 : (lane + 1) * 128]
        for piece in range(tile // per):
            sums[(tile // per) * step + piece] = lanes[piece * 8 : (piece + 1) * 8, :]

    send_summaries()

    def sum_copy(number, dy, pf, ps):
        return pltpu.make_async_remote_copy(
            src_ref=sums.at[4 * dy + ps],
            dst_ref=gathered.at[number],
            send_sem=sum_send.at[number],
            recv_sem=sum_arrive.at[number],
            device_id=(pf, ps),
            device_id_type=mesh_id,
        )

    for number, (dy, ds, pf, ps) in enumerate(peers):
        sum_copy(number, dy, pf, ps).start()
    total = sums[s]
    for number, (dy, ds, pf, ps) in enumerate(peers):
        sum_copy(number, dy, pf, ps).wait_recv()
        total = total + gathered[number]
    out_ref[...] = total
    for number in range(3):
        seq_copy(number).wait_recv()
    every_ref[...] = every[...]
    for number in range(7):
        turned_copy(number).wait_send()
        pools_copy(number).wait_send()
        parts_copy(number).wait_send()
    for number in range(3):
        seq_copy(number).wait_send()

    @pl.when(c == y)
    def _():
        head_copy(0).wait_send()

    for half in range(2):
        @pl.when(jnp.logical_not(is_self(half)))
        def _():
            for part in range(2):
                first(half, part).wait_send()
    for chunk in range(chunks):
        tok_across(chunk).wait_send()
        tok_over(chunk).wait_send()
    for distance, flip in order:
        turn(distance, flip, True)
    for number, (dy, ds, pf, ps) in enumerate(peers):
        sum_copy(number, dy, pf, ps).wait_send()


def plane(
    draft_tokens, draft_gate, draft_up, draft_head, normed, key_weight, value_weight,
    pool_query, flags, owner,
):
    rows, width = draft_tokens.shape
    segs = flags.shape[0]
    lanes = pool_query.shape[0]
    depth = key_weight.shape[0]
    turned = query_rows(key_weight, pool_query)
    pick = (jnp.repeat(owner, SEGL)[None, :] == jnp.arange(lanes, dtype=jnp.int32)[:, None])
    pick = jnp.repeat(pick.astype(jnp.float32), KVH, axis=0)
    live = jnp.broadcast_to(flags.astype(jnp.float32)[:, None], (segs, 128))
    head = jnp.broadcast_to(draft_head[None, :], (8, draft_head.shape[0]))
    packed = 2 * KVH * HD + 128
    sems = pltpu.SemaphoreType.DMA
    tiles, every = pl.pallas_call(
        plane_kernel_body,
        out_shape=(
            jax.ShapeDtypeStruct((8, 128), jnp.float32),
            jax.ShapeDtypeStruct((4, segs, packed), jnp.float32),
        ),
        in_specs=[pl.BlockSpec(memory_space=pl.ANY)] * 3
        + [pl.BlockSpec(memory_space=pltpu.VMEM)] * 7,
        out_specs=(pl.BlockSpec(memory_space=pltpu.VMEM),) * 2,
        scratch_shapes=[
            pltpu.VMEM((2 * rows, width), jnp.bfloat16),
            pltpu.VMEM((width, WIDE), jnp.bfloat16),
            pltpu.VMEM((width, WIDE), jnp.bfloat16),
            pltpu.VMEM((8, 8, 128), jnp.float32),
            pltpu.VMEM((7, 8, 128), jnp.float32),
            pltpu.VMEM((8, WIDE), jnp.float32),
            pltpu.VMEM((8, lanes * KVH, depth), jnp.float32),
            pltpu.VMEM((7, KVH * segs, depth), jnp.bfloat16),
            pltpu.VMEM((8, KVH * segs, depth), jnp.bfloat16),
            pltpu.VMEM((8, segs, packed - 128), jnp.float32),
            pltpu.VMEM((8, segs, packed - 128), jnp.float32),
            pltpu.VMEM((4, segs, packed), jnp.float32),
            sems,
            sems((2, 2)),
            sems((8, 2)),
            sems((8, 2)),
            sems((8, 2)),
            sems((2, 4)),
            sems((2, 4)),
            sems((7,)),
            sems((7,)),
            sems,
            sems,
            sems((3, 7)),
            sems((3, 7)),
            sems((3,)),
            sems((3,)),
        ],
        compiler_params=pltpu.CompilerParams(
            collective_id=0, has_side_effects=True, vmem_limit_bytes=48 * 1024 * 1024
        ),
        cost_estimate=pl.CostEstimate(
            flops=4 * 2 * rows * width * WIDE,
            bytes_accessed=24 * 1024 * 1024,
            transcendentals=2 * rows * WIDE,
        ),
    )(
        draft_tokens, draft_gate, draft_up, head, normed, turned, pick, live,
        key_weight, value_weight,
    )
    return jnp.sum(tiles, axis=1) / SEGL, every


def local(
    plane_kernel,
    draft_tokens,
    draft_gate,
    draft_up,
    draft_head,
    verifier_rows,
    norm_gain,
    key_weight,
    value_weight,
    pool_query,
    flags,
    owner,
):
    seg_count = flags.shape[0]
    normed = normalize_rows(verifier_rows, norm_gain)
    width = KVH * HD
    if plane_kernel:
        draft_score, every = plane(
            draft_tokens, draft_gate, draft_up, draft_head, normed, key_weight, value_weight,
            pool_query, flags, owner,
        )
        own = every[lax.axis_index("seq")]
        summary_key = own[:, :width].reshape(seg_count, KVH, HD)
        every = every.reshape(4 * seg_count, 2 * width + 128)
    else:
        draft_score = draft_gathered(draft_tokens, draft_gate, draft_up, draft_head, seg_count)
        summary_key, summary_value = pooled_summaries(
            normed, key_weight, value_weight, pool_query, owner
        )
        packed = jnp.concatenate(
            [
                summary_key.reshape(seg_count, width),
                summary_value.reshape(seg_count, width),
                jnp.broadcast_to(flags.astype(jnp.float32)[:, None], (seg_count, 128)),
            ],
            axis=1,
        )
        every = lax.all_gather(packed, "seq", axis=0, tiled=True)
    pooled = cross_pool(
        summary_key,
        every[:, :width].reshape(-1, KVH, HD),
        every[:, width : 2 * width].reshape(-1, KVH, HD),
        every[:, 2 * width] > 0.5,
        HD,
    )
    own_pooled = pooled.reshape(seg_count, KVH * HD)
    verdict = jnp.where(
        flags[:, None] == 1, jax.nn.sigmoid(draft_score)[:, None] * own_pooled, 0.0
    ).astype(jnp.bfloat16)
    return (draft_score, verdict)


def solution(mesh):
    plane_kernel = dict(mesh.shape) == {"fsdp": 2 * DEPTHS, "seq": 4}
    return jax.shard_map(
        functools.partial(local, plane_kernel),
        mesh=mesh,
        in_specs=(
            P("fsdp", None),
            P("fsdp", "seq"),
            P("fsdp", "seq"),
            P("seq"),
            P(("fsdp", "seq"), None),
            P(),
            P("fsdp", None),
            P("fsdp", None),
            P(),
            P(("fsdp", "seq")),
            P(("fsdp", "seq")),
        ),
        out_specs=(P(("fsdp", "seq")), P(("fsdp", "seq"), None)),
        check_vma=False,
    )
```

```python
import functools
import math

import jax
import jax.numpy as jnp
from jax import lax
from jax.experimental import pallas as pl
from jax.experimental.pallas import tpu as pltpu
from jax.sharding import PartitionSpec as P

KVH = 4
HD = 128
SEGL = 32


eps = 1e-05


def normalize_rows(rows, norm_gain):
    values = rows.astype(jnp.float32)
    scale = lax.rsqrt(jnp.mean(values * values, axis=-1, keepdims=True) + eps)
    return (values * scale * norm_gain).astype(jnp.bfloat16)


def split_pair(values):
    high = lax.reduce_precision(values, 8, 7)
    return high.astype(jnp.bfloat16), (values - high).astype(jnp.bfloat16)


def query_rows(key_weight, pool_query):
    depth = key_weight.shape[0]
    return jnp.einsum(
        "chk,dhk->chd",
        pool_query,
        key_weight.reshape(depth, KVH, HD).astype(jnp.float32),
        precision=lax.Precision.HIGHEST,
    ).reshape(pool_query.shape[0] * KVH, depth) / math.sqrt(HD)


def pooled_summaries(normed, key_weight, value_weight, pool_query, owner):
    lanes = pool_query.shape[0]
    segs = owner.shape[0]
    groups = lax.axis_size("fsdp")
    depth = key_weight.shape[0]
    key_heads = key_weight.reshape(depth, KVH, HD)
    value_heads = value_weight.reshape(depth, KVH, HD)
    turned = query_rows(key_weight, pool_query)
    turned = lax.all_gather(turned, "fsdp", axis=0)
    turned = turned.transpose(1, 0, 2).reshape(lanes * KVH, groups * depth)
    both = lax.dot_general(
        normed,
        jnp.concatenate(split_pair(turned), axis=0),
        (((1,), (1,)), ((), ())),
        preferred_element_type=jnp.float32,
    )
    scores = (both[:, : lanes * KVH] + both[:, lanes * KVH :]).reshape(segs, SEGL, lanes, KVH)
    pick = owner[:, None] == jnp.arange(lanes, dtype=jnp.int32)[None, :]
    scores = jnp.sum(jnp.where(pick[:, None, :, None], scores, 0.0), axis=2)
    scores = scores - jnp.max(scores, axis=1, keepdims=True)
    weights = jnp.exp(scores)
    weights = weights / jnp.sum(weights, axis=1, keepdims=True)
    spread = jnp.eye(segs, dtype=jnp.float32)[:, None, :, None] * jnp.transpose(
        weights, (2, 0, 1)
    ).transpose(1, 0, 2)[:, :, None, :]
    spread = spread.reshape(segs * KVH, segs * SEGL)
    high, low = split_pair(spread)
    pools = jnp.dot(jnp.concatenate([high, low], axis=0), normed, preferred_element_type=jnp.float32)
    pools = (pools[: segs * KVH] + pools[segs * KVH :]).astype(jnp.bfloat16)
    pools = pools.reshape(segs * KVH, groups, depth).transpose(1, 0, 2)
    pools = lax.all_to_all(pools, "fsdp", 0, 0).reshape(groups * segs, KVH, depth)
    partial = jnp.stack(
        [
            jnp.einsum("ghd,dhk->ghk", pools, heads, preferred_element_type=jnp.float32)
            for heads in (key_heads, value_heads)
        ]
    ).reshape(2, groups, segs, KVH * HD)
    partial = lax.all_to_all(partial.transpose(1, 0, 2, 3), "fsdp", 0, 0)
    summaries = jnp.sum(partial, axis=0).reshape(2, segs, KVH, HD)
    return summaries[0], summaries[1]


def cross_pool(query_keys, key_all, value_all, live_all, head_size):
    scores = jnp.einsum(
        "jhd,ihd->jhi", query_keys, key_all, precision=lax.Precision.HIGHEST
    ) / math.sqrt(head_size)
    scores = jnp.where(live_all[None, None, :], scores, -1e30)
    highest = jnp.max(scores, axis=2, keepdims=True)
    weights = jnp.where(live_all[None, None, :], jnp.exp(scores - highest), 0.0)
    total = jnp.sum(weights, axis=2, keepdims=True)
    return jnp.einsum("jhi,ihd->jhd", weights, value_all, precision=lax.Precision.HIGHEST) / total


def project_pair(row_block, pieces):
    return (
        jnp.dot(row_block, pieces[0], preferred_element_type=jnp.float32),
        jnp.dot(row_block, pieces[1], preferred_element_type=jnp.float32),
    )


def draft_gathered(draft_tokens, draft_gate, draft_up, draft_head, seg_count):
    gate, upward = project_pair(
        draft_tokens,
        (
            lax.all_gather(draft_gate, "fsdp", axis=0, tiled=True),
            lax.all_gather(draft_up, "fsdp", axis=0, tiled=True),
        ),
    )
    partial_scores = jnp.sum(jax.nn.silu(gate) * upward * draft_head[None, :], axis=1)
    own_scores = lax.psum_scatter(partial_scores, "seq", scatter_dimension=0, tiled=True)
    return jnp.mean(own_scores.reshape(seg_count, SEGL), axis=1)


DEPTHS = 4
WIDE = 512


def plane_kernel_body(
    tok_hbm, gate_hbm, up_hbm, head_in, normed, turned, pick, live, kw, vw,
    out_ref, every_ref,
    tok, wg, wu, sums, gathered, head_ref, every_turned, out_pools, pools, parts, back, every,
    tok_sem, first_send, near_send, far_send, arrive,
    tok_send, tok_arrive, sum_send, sum_arrive,
    head_send, head_arrive, col_send, col_arrive, seq_send, seq_arrive,
):
    f = lax.axis_index("fsdp")
    s = lax.axis_index("seq")
    z, y = f // 2, f % 2
    x, c = s // 2, s % 2
    weights = (wg, wu)
    rows = tok_hbm.shape[0]
    depth = gate_hbm.shape[0]
    mesh_id = pl.DeviceIdType.MESH

    barrier = pltpu.get_barrier_semaphore()
    peers = []
    for dy in range(2):
        for ds in range(4):
            if dy or ds:
                peers.append((dy, ds, 2 * z + lax.rem(y + dy, 2), lax.rem(s + ds, 4)))
    columns = [lax.rem(f + d, 8) for d in range(1, 8)]
    for _, _, pf, ps in peers:
        pl.semaphore_signal(barrier, inc=1, device_id=(pf, ps), device_id_type=mesh_id)
    for cf in columns:
        @pl.when(cf // 2 != z)
        def _():
            pl.semaphore_signal(barrier, inc=1, device_id=(cf, s), device_id_type=mesh_id)

    pl.semaphore_wait(barrier, 13)

    def column_copy(kind, number, source, target):
        return pltpu.make_async_remote_copy(
            src_ref=source,
            dst_ref=target,
            send_sem=col_send.at[kind, number],
            recv_sem=col_arrive.at[kind, number],
            device_id=(columns[number], s),
            device_id_type=mesh_id,
        )

    def turned_copy(number):
        return column_copy(0, number, turned, every_turned.at[f])

    def pools_copy(number):
        return column_copy(1, number, out_pools.at[number], pools.at[f])

    def parts_copy(number):
        return column_copy(2, number, parts.at[columns[number]], back.at[f])

    def seq_copy(number):
        return pltpu.make_async_remote_copy(
            src_ref=every.at[s],
            dst_ref=every.at[s],
            send_sem=seq_send.at[number],
            recv_sem=seq_arrive.at[number],
            device_id=(f, lax.rem(s + number + 1, 4)),
            device_id_type=mesh_id,
        )

    def head_copy(half):
        return pltpu.make_async_remote_copy(
            src_ref=head_in.at[:, half * WIDE : (half + 1) * WIDE],
            dst_ref=head_ref,
            send_sem=head_send,
            recv_sem=head_arrive,
            device_id=(f, 2 * x + half),
            device_id_type=mesh_id,
        )

    for half in range(2):
        @pl.when(jnp.logical_and(c == y, c != half))
        def _():
            head_copy(half).start()

        @pl.when(jnp.logical_and(c == y, c == half))
        def _():
            head_ref[...] = head_in[:, half * WIDE : (half + 1) * WIDE]

    for number in range(7):
        turned_copy(number).start()
    every_turned[f] = turned[...]

    segs = 8
    reach = kw.shape[0]
    width = KVH * HD

    def send_pools():
        for number in range(7):
            turned_copy(number).wait_recv()
        both = jnp.zeros((32, segs * SEGL), jnp.float32)
        for j in range(8):
            values = every_turned[j]
            high = values.astype(jnp.bfloat16)
            low = (values - high.astype(jnp.float32)).astype(jnp.bfloat16)
            both = both + lax.dot_general(
                jnp.concatenate([high, low], axis=0),
                normed[:, j * reach : (j + 1) * reach],
                (((1,), (1,)), ((), ())),
                preferred_element_type=jnp.float32,
            )
        scores = (both[:16] + both[16:]) * pick[...]
        scores = jnp.sum(scores.reshape(4, KVH, segs * SEGL), axis=0)
        wide = jnp.concatenate(
            [jnp.broadcast_to(scores[h : h + 1], (segs, segs * SEGL)) for h in range(KVH)],
            axis=0,
        )
        row = lax.broadcasted_iota(jnp.int32, wide.shape, 0) % segs
        inside = lax.broadcasted_iota(jnp.int32, wide.shape, 1) // SEGL == row
        wide = jnp.where(inside, wide, -1e30)
        shares = jnp.where(inside, jnp.exp(wide - jnp.max(wide, axis=1, keepdims=True)), 0.0)
        shares = shares / jnp.sum(shares, axis=1, keepdims=True)
        high = shares.astype(jnp.bfloat16)
        low = (shares - high.astype(jnp.float32)).astype(jnp.bfloat16)
        pair = jnp.concatenate([high, low], axis=0)

        def pool(j):
            block = normed[:, pl.ds(pl.multiple_of(j * reach, reach), reach)]
            result = jnp.dot(pair, block, preferred_element_type=jnp.float32)
            return (result[:32] + result[32:]).astype(jnp.bfloat16)

        for number in range(7):
            out_pools[number] = pool(columns[number])
            pools_copy(number).start()
        pools[f] = pool(f)

    def send_parts():
        for number in range(7):
            pools_copy(number).wait_recv()
        block = pools[...].reshape(8 * 32, reach)
        for which, ref in enumerate((kw, vw)):
            result = jnp.dot(block, ref[...], preferred_element_type=jnp.float32)
            result = result.reshape(8, KVH, segs, width)
            for h in range(KVH):
                start = which * width + h * HD
                parts[:, :, start : start + HD] = result[:, h, :, h * HD : (h + 1) * HD]
        for number in range(7):
            parts_copy(number).start()
        back[f] = parts[f]

    def send_summaries():
        for number in range(7):
            parts_copy(number).wait_recv()
        every[s] = jnp.concatenate([jnp.sum(back[...], axis=0), live[...]], axis=1)
        for number in range(3):
            seq_copy(number).start()

    def slot(ref, index):
        return ref.at[pl.ds(pl.multiple_of(index * depth, depth), depth), :]

    def first(half, part):
        source = (gate_hbm, up_hbm)[part].at[:, half * WIDE : (half + 1) * WIDE]
        return pltpu.make_async_remote_copy(
            src_ref=source,
            dst_ref=slot(weights[part], f),
            send_sem=first_send.at[half, part],
            recv_sem=arrive.at[f, part],
            device_id=(2 * z + c, 2 * x + half),
            device_id_type=mesh_id,
        )

    def kept(half, part):
        source = (gate_hbm, up_hbm)[part].at[:, half * WIDE : (half + 1) * WIDE]
        return pltpu.make_async_copy(source, slot(weights[part], f), arrive.at[f, part])

    def is_self(half):
        return jnp.logical_and(c == y, c == half)

    for half in range(2):
        @pl.when(jnp.logical_not(is_self(half)))
        def _():
            for part in range(2):
                first(half, part).start()

        @pl.when(is_self(half))
        def _():
            for part in range(2):
                kept(half, part).start()

    other_f = 2 * z + 1 - y
    chunks = 4
    size = rows // 2 // chunks

    def chunk_rows(core, chunk):
        return pl.multiple_of(core * (rows // 2) + chunk * size, size)

    def tok_across(chunk):
        start = chunk_rows(c, chunk)
        return pltpu.make_async_remote_copy(
            src_ref=tok_hbm.at[pl.ds(start, size), :],
            dst_ref=tok.at[pl.ds(rows + start, size), :],
            send_sem=tok_send.at[0, chunk],
            recv_sem=tok_arrive.at[0, chunk],
            device_id=(other_f, s),
            device_id_type=mesh_id,
        )

    def tok_over(chunk):
        start = rows + chunk_rows(c, chunk)
        return pltpu.make_async_remote_copy(
            src_ref=tok.at[pl.ds(start, size), :],
            dst_ref=tok.at[pl.ds(start, size), :],
            send_sem=tok_send.at[1, chunk],
            recv_sem=tok_arrive.at[1, chunk],
            device_id=(f, 2 * x + 1 - c),
            device_id_type=mesh_id,
        )

    own_tokens = pltpu.make_async_copy(tok_hbm, tok.at[pl.ds(0, rows), :], tok_sem)
    own_tokens.start()

    def forward(index, part, step):
        sems = near_send if step < 0 else far_send
        return pltpu.make_async_remote_copy(
            src_ref=slot(weights[part], index),
            dst_ref=slot(weights[part], index),
            send_sem=sems.at[index, part],
            recv_sem=arrive.at[index, part],
            device_id=(f + 2 * step, s),
            device_id_type=mesh_id,
        )

    def arrived(index):
        for part in range(2):
            forward(index, part, 1).wait_recv()

    def both(index, step, wait):
        for part in range(2):
            if wait:
                forward(index, part, step).wait_send()
            else:
                forward(index, part, step).start()

    def turn(distance, flip, wait):
        side = y if flip == 0 else 1 - y
        if distance == 0:
            index = f if flip == 0 else other_f
            if not wait:
                arrived(index)

            @pl.when(z < DEPTHS - 1)
            def _():
                both(index, 1, wait)

            @pl.when(z > 0)
            def _():
                both(index, -1, wait)

            return

        @pl.when(z >= distance)
        def _():
            index = 2 * (z - distance) + side
            if not wait:
                arrived(index)

            @pl.when(z < DEPTHS - 1)
            def _():
                both(index, 1, wait)

        @pl.when(z + distance < DEPTHS)
        def _():
            index = 2 * (z + distance) + side
            if not wait:
                arrived(index)

            @pl.when(z > 0)
            def _():
                both(index, -1, wait)

    order = ((0, 0), (1, 0), (0, 1), (2, 0), (1, 1), (3, 0), (2, 1), (3, 1))
    for number, (distance, flip) in enumerate(order):
        turn(distance, flip, False)
        if number == 1:
            send_pools()
            for chunk in range(chunks):
                tok_across(chunk).start()
        if number == 3:
            send_parts()
        if number == 5:
            send_summaries()
    for chunk in range(chunks):
        tok_across(chunk).wait_recv()
        tok_over(chunk).start()
    for chunk in range(chunks):
        tok_over(chunk).wait_recv()
    own_tokens.wait()

    tile = 512
    per = rows // 4

    @pl.when(c != y)
    def _():
        head_copy(0).wait_recv()

    head = head_ref[0:1, :]

    @pl.loop(0, 2 * rows // tile)
    def _(step):
        block = tok[pl.ds(pl.multiple_of(step * tile, tile), tile), :]
        gate = jnp.dot(block, wg[...], preferred_element_type=jnp.float32)
        upward = jnp.dot(block, wu[...], preferred_element_type=jnp.float32)
        product = gate / (1.0 + jnp.exp(-gate)) * upward * head
        by_seg = jnp.sum(product.reshape(tile // SEGL, SEGL, WIDE), axis=1)
        lanes = by_seg[:, 0:128]
        for lane in range(1, WIDE // 128):
            lanes = lanes + by_seg[:, lane * 128 : (lane + 1) * 128]
        for piece in range(tile // per):
            sums[(tile // per) * step + piece] = lanes[piece * 8 : (piece + 1) * 8, :]

    def sum_copy(number, dy, pf, ps):
        return pltpu.make_async_remote_copy(
            src_ref=sums.at[4 * dy + ps],
            dst_ref=gathered.at[number],
            send_sem=sum_send.at[number],
            recv_sem=sum_arrive.at[number],
            device_id=(pf, ps),
            device_id_type=mesh_id,
        )

    for number, (dy, ds, pf, ps) in enumerate(peers):
        sum_copy(number, dy, pf, ps).start()
    total = sums[s]
    for number, (dy, ds, pf, ps) in enumerate(peers):
        sum_copy(number, dy, pf, ps).wait_recv()
        total = total + gathered[number]
    out_ref[...] = total
    for number in range(3):
        seq_copy(number).wait_recv()
    every_ref[...] = every[...]
    for number in range(7):
        turned_copy(number).wait_send()
        pools_copy(number).wait_send()
        parts_copy(number).wait_send()
    for number in range(3):
        seq_copy(number).wait_send()

    @pl.when(c == y)
    def _():
        head_copy(0).wait_send()

    for half in range(2):
        @pl.when(jnp.logical_not(is_self(half)))
        def _():
            for part in range(2):
                first(half, part).wait_send()
    for chunk in range(chunks):
        tok_across(chunk).wait_send()
        tok_over(chunk).wait_send()
    for distance, flip in order:
        turn(distance, flip, True)
    for number, (dy, ds, pf, ps) in enumerate(peers):
        sum_copy(number, dy, pf, ps).wait_send()


def plane(
    draft_tokens, draft_gate, draft_up, draft_head, normed, key_weight, value_weight,
    pool_query, flags, owner,
):
    rows, width = draft_tokens.shape
    segs = flags.shape[0]
    lanes = pool_query.shape[0]
    depth = key_weight.shape[0]
    turned = query_rows(key_weight, pool_query)
    pick = (jnp.repeat(owner, SEGL)[None, :] == jnp.arange(lanes, dtype=jnp.int32)[:, None])
    pick = jnp.repeat(pick.astype(jnp.float32), KVH, axis=0)
    live = jnp.broadcast_to(flags.astype(jnp.float32)[:, None], (segs, 128))
    head = jnp.broadcast_to(draft_head[None, :], (8, draft_head.shape[0]))
    packed = 2 * KVH * HD + 128
    sems = pltpu.SemaphoreType.DMA
    tiles, every = pl.pallas_call(
        plane_kernel_body,
        out_shape=(
            jax.ShapeDtypeStruct((8, 128), jnp.float32),
            jax.ShapeDtypeStruct((4, segs, packed), jnp.float32),
        ),
        in_specs=[pl.BlockSpec(memory_space=pl.ANY)] * 3
        + [pl.BlockSpec(memory_space=pltpu.VMEM)] * 7,
        out_specs=(pl.BlockSpec(memory_space=pltpu.VMEM),) * 2,
        scratch_shapes=[
            pltpu.VMEM((2 * rows, width), jnp.bfloat16),
            pltpu.VMEM((width, WIDE), jnp.bfloat16),
            pltpu.VMEM((width, WIDE), jnp.bfloat16),
            pltpu.VMEM((8, 8, 128), jnp.float32),
            pltpu.VMEM((7, 8, 128), jnp.float32),
            pltpu.VMEM((8, WIDE), jnp.float32),
            pltpu.VMEM((8, lanes * KVH, depth), jnp.float32),
            pltpu.VMEM((7, KVH * segs, depth), jnp.bfloat16),
            pltpu.VMEM((8, KVH * segs, depth), jnp.bfloat16),
            pltpu.VMEM((8, segs, packed - 128), jnp.float32),
            pltpu.VMEM((8, segs, packed - 128), jnp.float32),
            pltpu.VMEM((4, segs, packed), jnp.float32),
            sems,
            sems((2, 2)),
            sems((8, 2)),
            sems((8, 2)),
            sems((8, 2)),
            sems((2, 4)),
            sems((2, 4)),
            sems((7,)),
            sems((7,)),
            sems,
            sems,
            sems((3, 7)),
            sems((3, 7)),
            sems((3,)),
            sems((3,)),
        ],
        compiler_params=pltpu.CompilerParams(
            collective_id=0, has_side_effects=True, vmem_limit_bytes=48 * 1024 * 1024
        ),
        cost_estimate=pl.CostEstimate(
            flops=4 * 2 * rows * width * WIDE,
            bytes_accessed=24 * 1024 * 1024,
            transcendentals=2 * rows * WIDE,
        ),
    )(
        draft_tokens, draft_gate, draft_up, head, normed, turned, pick, live,
        key_weight, value_weight,
    )
    return jnp.sum(tiles, axis=1) / SEGL, every


def local(
    plane_kernel,
    draft_tokens,
    draft_gate,
    draft_up,
    draft_head,
    verifier_rows,
    norm_gain,
    key_weight,
    value_weight,
    pool_query,
    flags,
    owner,
):
    seg_count = flags.shape[0]
    normed = normalize_rows(verifier_rows, norm_gain)
    width = KVH * HD
    if plane_kernel:
        draft_score, every = plane(
            draft_tokens, draft_gate, draft_up, draft_head, normed, key_weight, value_weight,
            pool_query, flags, owner,
        )
        own = every[lax.axis_index("seq")]
        summary_key = own[:, :width].reshape(seg_count, KVH, HD)
        every = every.reshape(4 * seg_count, 2 * width + 128)
    else:
        draft_score = draft_gathered(draft_tokens, draft_gate, draft_up, draft_head, seg_count)
        summary_key, summary_value = pooled_summaries(
            normed, key_weight, value_weight, pool_query, owner
        )
        packed = jnp.concatenate(
            [
                summary_key.reshape(seg_count, width),
                summary_value.reshape(seg_count, width),
                jnp.broadcast_to(flags.astype(jnp.float32)[:, None], (seg_count, 128)),
            ],
            axis=1,
        )
        every = lax.all_gather(packed, "seq", axis=0, tiled=True)
    pooled = cross_pool(
        summary_key,
        every[:, :width].reshape(-1, KVH, HD),
        every[:, width : 2 * width].reshape(-1, KVH, HD),
        every[:, 2 * width] > 0.5,
        HD,
    )
    own_pooled = pooled.reshape(seg_count, KVH * HD)
    verdict = jnp.where(
        flags[:, None] == 1, jax.nn.sigmoid(draft_score)[:, None] * own_pooled, 0.0
    ).astype(jnp.bfloat16)
    return (draft_score, verdict)


def solution(mesh):
    plane_kernel = dict(mesh.shape) == {"fsdp": 2 * DEPTHS, "seq": 4}
    return jax.shard_map(
        functools.partial(local, plane_kernel),
        mesh=mesh,
        in_specs=(
            P("fsdp", None),
            P("fsdp", "seq"),
            P("fsdp", "seq"),
            P("seq"),
            P(("fsdp", "seq"), None),
            P(),
            P("fsdp", None),
            P("fsdp", None),
            P(),
            P(("fsdp", "seq")),
            P(("fsdp", "seq")),
        ),
        out_specs=(P(("fsdp", "seq")), P(("fsdp", "seq"), None)),
        check_vma=False,
    )
```
